32 devices in a mesh: groups: 2 (over y), dom: 4 (over z), blk: 4 (over x, core).
Axes of the slice: x: 2, y: 2, z: 4, core: 2. Of those that a mesh axis runs over, the one named last changes fastest.
Arguments:
- features: bfloat16 [16384, 128], P(('groups', 'dom', 'blk')), parts along dimension 0, may hold values from -6 to 6
- weight: bfloat16 [128, 256], replicated, may hold values from -0.5 to 0.5
- tiles: bfloat16 [8, 4, 19, 128, 128], P(('groups', 'dom'), 'blk'), parts along dimension 0, may hold values from -0.25 to 0.25
- tile_rows: int32 [8, 4, 19], P(('groups', 'dom'), 'blk'), parts along dimension 0, may hold values from 0 to 15
- tile_sources: int32 [8, 4, 19], P(('groups', 'dom'), 'blk'), parts along dimension 0, may hold values from 0 to 7, as said below
- send_blocks: int32 [8, 4, 4], P(('groups', 'dom'), 'blk'), parts along dimension 0, may hold values from 0 to 4, as said below
- cotangent: bfloat16 [16384, 256], P(('groups', 'dom', 'blk')), parts along dimension 0, may hold values from -6 to 6
Outputs:
- activations: bfloat16 [16384, 256], P(('groups', 'dom', 'blk')), parts along dimension 0
- feature_grad: bfloat16 [16384, 128], P(('groups', 'dom', 'blk')), parts along dimension 0
- weight_grad: float32 [256, 256], P('groups'), parts along dimension 0
The draws below stay inside these ranges and needn't reach their ends.
There are 2 independent parts, one for each index of `groups`. The reference program is written for one: setup_inputs(seed, part) draws one part's arguments, and reference() takes and returns one part's arrays. A program takes and returns all parts, laid end to end along the dimension named above; an argument that names none is the same for every part. Nothing has to cross between parts.
Inputs may be any that keep to these rules, and one draw needn't show every extreme that they name: `send_blocks`: entry [e, b, d] names the row block of device (e, b) that domain d reads, counted within that device's 4 blocks; 4 means none. Entry [d, b, d] is always 4. A domain reads from at most 3 other domains. `tile_sources`: slot s below 4 is the device's own s-th row block; slot 4 + e is the block received from domain e and is named only where send_blocks[e, b, d] is below 4; every such received block is named by at least one tile of the reader.
All inputs are finite; a program needn't handle non-finite values.
Results may differ from the reference program's by a relative error of at most 0.0063.
Values may be sent and summed in bfloat16 or wider, within the bound.
A program may use at most 64 MiB of HBM per device.

```python
import math
import jax
import jax.numpy as jnp
from jax import lax

BS = 128
F = 128
HID = 256
RB = 4
HALO = 3
TILES = 19
DOMROWS = 16
NODES = 8192
N_DOM = 4
N_BLK = 4


def cycle_offsets():
    steps = jnp.arange(HALO)
    if HALO == N_DOM - 1:
        return steps + 1
    return jnp.maximum(1, steps * N_DOM // HALO)


def halo_usable(key):
    recv_rates = jax.random.randint(jax.random.fold_in(key, 11), (N_DOM, N_BLK, 1), 1, 9)
    dice_rolls = jax.random.randint(jax.random.fold_in(key, 12), (N_DOM, N_BLK, N_DOM), 0, 8)
    usable = dice_rolls < recv_rates
    receiver = jnp.arange(N_DOM)[:, None, None]
    sender = jnp.arange(N_DOM)[None, None, :]
    distance = (receiver - sender) % N_DOM
    offsets = cycle_offsets()
    allowed = jnp.any(distance[..., None] == offsets[None, None, None, :], axis=-1)
    usable = usable & allowed
    forced = (receiver == 0) & (sender == N_DOM - 1)
    return usable | forced


def draw_send_blocks(key, part):
    usable = halo_usable(key)
    key = jax.random.fold_in(key, 3)
    picked = jax.random.randint(key, (N_DOM, N_BLK, N_DOM), 0, RB)
    usable_sender = jnp.transpose(usable, (2, 1, 0))
    return jnp.where(usable_sender, picked, RB).astype(jnp.int32)


def draw_tile_sources(key, part):
    usable = halo_usable(key)
    key = jax.random.fold_in(key, 5)
    key_own, key_extra, key_mix, key_order = jax.random.split(key, 4)
    shape = (N_DOM, N_BLK, TILES)
    own_slots = jax.random.randint(key_own, shape, 0, RB)
    extra_slots = jax.random.randint(key_extra, shape, RB, RB + N_DOM)
    mixing = jax.random.randint(key_mix, shape, 0, 2)
    position = jnp.arange(TILES)[None, None, :]
    receiver = jnp.arange(N_DOM)[:, None, None]
    offsets = cycle_offsets()
    offset_at = offsets[jnp.minimum(position, HALO - 1)]
    near_sender = (receiver - offset_at) % N_DOM
    proposed = jnp.where(position < HALO, RB + near_sender, jnp.where(mixing == 1, extra_slots, own_slots))
    sender = jnp.clip(proposed - RB, 0, N_DOM - 1)
    allowed = jnp.take_along_axis(usable, sender, axis=2) & (proposed >= RB)
    sources = jnp.where(allowed, proposed, own_slots)
    scores = jax.random.randint(key_order, shape, 0, 1 << 30)
    ordering = jnp.argsort(scores, axis=2, stable=True)
    return jnp.take_along_axis(sources, ordering, axis=2).astype(jnp.int32)


def set_ends(entries, own_key, low, top_value):
    index_at = [jax.random.randint(jax.random.fold_in(own_key, axis), (), 0, length) for axis, length in enumerate(entries.shape)]
    longest = entries.shape.index(max(entries.shape))
    neighbour = index_at[:longest] + [(index_at[longest] + 1) % entries.shape[longest]] + index_at[longest + 1:]
    return entries.at[tuple(index_at)].set(low).at[tuple(neighbour)].set(top_value)


def block_scale(rng, extent, pieces, smallest, largest):
    gain = 1.0
    for dim, shards_of in pieces:
        steps = jax.random.uniform(jax.random.fold_in(jax.random.fold_in(rng, 6), dim), (shards_of,), jnp.float32, smallest / len(pieces), largest / len(pieces))
        gain = gain * jnp.repeat(jnp.exp(steps), extent[dim] // shards_of).reshape((-1,) + (1,) * (len(extent) - 1 - dim))
    return gain


def normal_values(own_key, dims, width, reach, cuts=(), kind=jnp.bfloat16):
    loudness = block_scale(own_key, dims, cuts, -0.22, 0.18) if cuts else 1.0
    result = jax.random.normal(own_key, dims, jnp.float32) * width * loudness
    return jnp.minimum(jnp.maximum(result, -reach), reach).astype(kind)


def setup_inputs(seed: int = 0, part: int = 0) -> dict:
    splits = jax.random.split(jax.random.key(seed), 8)
    part_splits = jax.random.split(jax.random.fold_in(splits[7], part), 8)
    features = normal_values(part_splits[0], (NODES, F), 1.0, 6.0, ((0, 16),))
    weight = normal_values(splits[1], (F, HID), F ** -0.5, 0.5)
    tiles = normal_values(part_splits[2], (N_DOM, N_BLK, TILES, BS, BS), (BS * TILES // RB) ** -0.5, 0.25, ((0, 4), (1, 4)))
    tile_rows = set_ends(jax.random.randint(part_splits[3], (N_DOM, N_BLK, TILES), 0, DOMROWS), jax.random.fold_in(part_splits[3], 1), 0, DOMROWS - 1).astype(jnp.int32)
    tile_sources = draw_tile_sources(jax.random.fold_in(jax.random.fold_in(splits[7], part), 71), part)
    send_blocks = draw_send_blocks(jax.random.fold_in(jax.random.fold_in(splits[7], part), 71), part)
    cotangent = normal_values(part_splits[6], (NODES, HID), 1.0, 6.0, ((0, 16),))
    return {"features": features, "weight": weight, "tiles": tiles, "tile_rows": tile_rows, "tile_sources": tile_sources, "send_blocks": send_blocks, "cotangent": cotangent}


def reference(features, weight, tiles, tile_rows, tile_sources, send_blocks, cotangent):
    num_blocks = N_DOM * N_BLK * RB
    projected = jnp.dot(features, weight, preferred_element_type=jnp.float32).astype(jnp.bfloat16)
    proj_wide = projected.astype(jnp.float32).reshape(num_blocks, BS, HID)
    devices = jnp.arange(N_DOM * N_BLK).astype(jnp.int32)
    domain_ids = jnp.arange(N_DOM).astype(jnp.int32)

    def locate(device):
        domain = device // N_BLK
        member = device % N_BLK
        sources = tile_sources[domain, member]
        sender = jnp.clip(sources - RB, 0, N_DOM - 1)
        picked = send_blocks[sender, member, domain]
        halo_ids = (sender * N_BLK + member) * RB + jnp.minimum(picked, RB - 1)
        own_ids = device * RB + jnp.minimum(sources, RB - 1)
        global_ids = jnp.where(sources < RB, own_ids, halo_ids).astype(jnp.int32)
        targets = (domain * (N_BLK * RB) + tile_rows[domain, member]).astype(jnp.int32)
        return (domain, member, sources, global_ids, targets)

    def forward_step(aggregated, device):
        domain, member, sources, global_ids, targets = locate(device)
        tile_mats = tiles[domain, member].astype(jnp.float32)
        contrib = jnp.einsum('tij,tjh->tih', tile_mats, proj_wide[global_ids])
        return (aggregated.at[targets].add(contrib), None)
    aggregated, _ = lax.scan(forward_step, jnp.zeros((num_blocks, BS, HID), jnp.float32), devices)
    aggregated = aggregated.reshape(NODES, HID)
    activations = jax.nn.silu(aggregated).astype(jnp.bfloat16)
    sigmoid_z = jax.nn.sigmoid(aggregated)
    pre_grad = (cotangent.astype(jnp.float32) * sigmoid_z * (1.0 + aggregated * (1.0 - sigmoid_z))).astype(jnp.bfloat16)
    pre_wide = pre_grad.astype(jnp.float32).reshape(num_blocks, BS, HID)

    def backward_step(grad_sum, device):
        domain, member, sources, global_ids, targets = locate(device)
        tile_mats = tiles[domain, member].astype(jnp.float32)
        back = jnp.einsum('tji,tjh->tih', tile_mats, pre_wide[targets])
        slot_sums = jnp.zeros((RB + N_DOM, BS, HID), jnp.float32).at[sources].add(back)
        own_slots = slot_sums[:RB]
        halo_slots = lax.optimization_barrier(slot_sums[RB:].astype(jnp.bfloat16)).astype(jnp.float32)
        own_ids = (device * RB + jnp.arange(RB)).astype(jnp.int32)
        grad_sum = grad_sum.at[own_ids].add(own_slots)
        picked = send_blocks[domain_ids, member, domain]
        usable = picked < RB
        halo_ids = ((domain_ids * N_BLK + member) * RB + jnp.minimum(picked, RB - 1)).astype(jnp.int32)
        grad_sum = grad_sum.at[halo_ids].add(jnp.where(usable[:, None, None], halo_slots, jnp.zeros_like(halo_slots)))
        return (grad_sum, None)
    grad_sum, _ = lax.scan(backward_step, jnp.zeros((num_blocks, BS, HID), jnp.float32), devices)
    projected_grad = grad_sum.reshape(NODES, HID).astype(jnp.bfloat16)
    weight_grad = jnp.dot(features.T, projected_grad, preferred_element_type=jnp.float32) / math.sqrt(NODES)
    feature_grad = jnp.dot(projected_grad, weight.T, preferred_element_type=jnp.float32).astype(jnp.bfloat16)
    return (activations, feature_grad, weight_grad)
```

```python
import functools
import math

import jax
import jax.numpy as jnp
from jax import lax
from jax.experimental import pallas as pl
from jax.experimental.pallas import tpu as pltpu
from jax.sharding import PartitionSpec as P

MESH = pl.DeviceIdType.MESH
BF16 = jnp.bfloat16
F32 = jnp.float32
DMA = pltpu.SemaphoreType.DMA


def each(low, high, step):
    if high - low <= 16:
        for i in range(low, high):
            step(i)
    else:
        lax.fori_loop(low, high, lambda i, c: (step(i), c)[1], 0)


def chain(keys, key_count, none):
    before = []
    for t, key in enumerate(keys):
        found = none
        for u in range(t):
            found = jnp.where(keys[u] == key, u, found)
        before.append(found)
    last = []
    for r in range(key_count):
        found = none
        for t, key in enumerate(keys):
            found = jnp.where(key == r, t, found)
        last.append(found)
    return before, last


def kernel(
    domains, members, sum_here, scale,
    rows_ref, sources_ref, chosen_ref, feat_hbm, weight_hbm, tiles_hbm, cot_hbm,
    act_hbm, fgrad_hbm, wgrad_hbm,
    feat, weight, tiles, tiles_t, cot, slots, outgoing, acc, last_ref, rs_out, rs_in, act, dom_h,
    ret_out, ret_in, fgrad, wpart, wparts, wgrad,
    local_sem, halo_send, halo_recv, rs_send, rs_recv, ag_send, ag_recv, ret_send, ret_recv,
    ws_send, ws_recv, wg_send, wg_recv,
):
    own, size, width = feat.shape
    count = tiles.shape[0]
    d = lax.axis_index("dom")
    b = lax.axis_index("blk")
    peers = domains * members
    me = d * members + b

    def dom_at(k):
        return lax.rem(d + k, domains)

    def blk_at(k):
        return lax.rem(b + k, members)

    def peer_at(k):
        index = lax.rem(me + k, peers)
        return index, {"dom": index // members, "blk": lax.rem(index, members)}

    loads = [
        pltpu.make_async_copy(feat_hbm, feat, local_sem.at[0]),
        pltpu.make_async_copy(feat_hbm, slots.at[pl.ds(0, own)], local_sem.at[1]),
        pltpu.make_async_copy(tiles_hbm.at[0, 0], tiles, local_sem.at[2]),
        pltpu.make_async_copy(weight_hbm, weight, local_sem.at[3]),
        pltpu.make_async_copy(cot_hbm, cot, local_sem.at[4]),
    ]
    for load in loads:
        load.start()

    barrier = pltpu.get_barrier_semaphore()
    if sum_here:
        each(1, peers, lambda k: pl.semaphore_signal(
            barrier, inc=1, device_id=peer_at(k)[1], device_id_type=MESH))
        waits = peers - 1
    else:
        each(1, domains, lambda k: pl.semaphore_signal(
            barrier, inc=1, device_id={"dom": dom_at(k)}, device_id_type=MESH))
        each(1, members, lambda k: pl.semaphore_signal(
            barrier, inc=1, device_id={"blk": blk_at(k)}, device_id_type=MESH))
        waits = domains + members - 2

    loads[0].wait()

    def pick(k):
        outgoing[k - 1] = feat[jnp.minimum(chosen_ref[0, 0, dom_at(k)], own - 1)]

    each(1, domains, pick)
    pl.semaphore_wait(barrier, waits)

    def halo(k):
        return pltpu.make_async_remote_copy(
            outgoing.at[k - 1], slots.at[own + d], halo_send.at[k - 1], halo_recv.at[k - 1],
            device_id={"dom": dom_at(k)}, device_id_type=MESH)

    def halo_in(k):
        return pltpu.make_async_remote_copy(
            outgoing.at[k - 1], slots.at[own + dom_at(domains - k)], halo_send.at[k - 1],
            halo_recv.at[k - 1], device_id={"dom": dom_at(k)}, device_id_type=MESH)

    each(1, domains, lambda k: halo(k).start())

    rows = [rows_ref[0, 0, t] for t in range(count)]
    sources = [sources_ref[0, 0, t] for t in range(count)]
    before, last = chain(rows, own * members, count)
    for r, value in enumerate(last):
        last_ref[r] = value
    acc[count] = jnp.zeros((size, width), F32)
    slots[own + d] = jnp.zeros((size, width), BF16)
    for load in loads[1:]:
        load.wait()
    each(1, domains, lambda k: halo_in(k).wait_recv())

    for t in range(count):
        product = jnp.dot(tiles[t], slots[sources[t]], preferred_element_type=F32)
        acc[t] = product + acc[before[t]]

    def scatter(m):
        return pltpu.make_async_remote_copy(
            rs_out.at[m - 1], rs_in.at[m - 1], rs_send.at[m - 1], rs_recv.at[m - 1],
            device_id={"blk": blk_at(m)}, device_id_type=MESH)

    for m in range(1, members):
        target = blk_at(m)
        for s in range(own):
            rs_out[m - 1, s] = acc[last_ref[target * own + s]].astype(BF16)
        scatter(m).start()

    own_rows = [acc[last_ref[b * own + s]] for s in range(own)]
    total = jnp.concatenate(own_rows, axis=0)

    before, last = chain(sources, own + domains, count)
    for t in range(count):
        tiles_t[t] = tiles[t].T

    for m in range(1, members):
        scatter(m).wait_recv()
        total = total + rs_in[m - 1].reshape(own * size, width).astype(F32)

    gathered = total.astype(BF16)
    z = jnp.dot(gathered, weight[...], preferred_element_type=F32)
    sig = jax.nn.sigmoid(z)
    grad = (cot[...].astype(F32) * sig * (1.0 + z * (1.0 - sig))).astype(BF16)
    h = lax.dot_general(
        grad, weight[...], (((1,), (1,)), ((), ())), preferred_element_type=F32).astype(BF16)
    dom_h[pl.ds(b * own, own)] = h.reshape(own, size, width)

    def spread(m):
        return pltpu.make_async_remote_copy(
            dom_h.at[pl.ds(b * own, own)], dom_h.at[pl.ds(b * own, own)], ag_send.at[m - 1],
            ag_recv.at[m - 1], device_id={"blk": blk_at(m)}, device_id_type=MESH)

    def spread_in(m):
        return pltpu.make_async_remote_copy(
            dom_h.at[pl.ds(b * own, own)], dom_h.at[pl.ds(blk_at(members - m) * own, own)],
            ag_send.at[m - 1], ag_recv.at[m - 1], device_id={"blk": blk_at(m)},
            device_id_type=MESH)

    for m in range(1, members):
        spread(m).start()

    act[...] = (z * sig).astype(BF16)
    stores = [pltpu.make_async_copy(act, act_hbm, local_sem.at[5])]
    stores[0].start()
    wpart[...] = lax.dot_general(
        gathered, grad, (((0,), (0,)), ((), ())), preferred_element_type=F32)
    piece = wpart.shape[0] // peers

    def wscatter(k):
        index, device = peer_at(k)
        return pltpu.make_async_remote_copy(
            wpart.at[pl.ds(pl.multiple_of(index * piece, 8), piece)], wparts.at[k - 1],
            ws_send.at[k - 1], ws_recv.at[k - 1], device_id=device, device_id_type=MESH)

    def wspread(k, who):
        piece_at = pl.ds(pl.multiple_of(who * piece, 8), piece)
        return pltpu.make_async_remote_copy(
            wgrad.at[piece_at], wgrad.at[piece_at], wg_send.at[k - 1], wg_recv.at[k - 1],
            device_id=peer_at(k)[1], device_id_type=MESH)

    if sum_here:
        each(1, peers, lambda k: wscatter(k).start())
    else:
        wgrad[...] = wpart[...] * scale

    for m in range(1, members):
        spread_in(m).wait_recv()
    for t in range(count):
        product = jnp.dot(tiles_t[t], dom_h[rows[t]], preferred_element_type=F32)
        acc[t] = product + acc[before[t]]
    for s, value in enumerate(last):
        last_ref[s] = value

    def give_back(k):
        return pltpu.make_async_remote_copy(
            ret_out.at[k - 1], ret_in.at[k - 1], ret_send.at[k - 1], ret_recv.at[k - 1],
            device_id={"dom": dom_at(k)}, device_id_type=MESH)

    def give(k):
        ret_out[k - 1] = acc[last_ref[own + dom_at(k)]].astype(BF16)
        give_back(k).start()

    each(1, domains, give)

    if sum_here:
        each(1, peers, lambda k: wscatter(k).wait_recv())
        mine = pl.ds(pl.multiple_of(me * piece, 8), piece)
        summed = wpart[mine, :]
        for k in range(1, peers):
            summed = summed + wparts[k - 1]
        wgrad[mine, :] = summed * scale
        each(1, peers, lambda k: wspread(k, me).start())

    for s in range(own):
        fgrad[s] = acc[last_ref[s]]

    def land(k):
        give_back(k).wait_recv()
        block = chosen_ref[0, 0, dom_at(domains - k)]
        value = ret_in[k - 1].astype(F32)
        for s in range(own):
            fgrad[s] += jnp.where(block == s, value, 0.0)

    each(1, domains, land)
    feat[...] = fgrad[...].astype(BF16)
    stores.append(pltpu.make_async_copy(feat, fgrad_hbm, local_sem.at[6]))
    stores[1].start()

    if sum_here:
        each(1, peers, lambda k: wspread(k, lax.rem(me + peers - k, peers)).wait_recv())
    stores.append(pltpu.make_async_copy(wgrad, wgrad_hbm, local_sem.at[7]))
    stores[2].start()

    each(1, domains, lambda k: halo(k).wait_send())
    each(1, domains, lambda k: give_back(k).wait_send())
    for m in range(1, members):
        scatter(m).wait_send()
        spread(m).wait_send()
    if sum_here:
        each(1, peers, lambda k: wscatter(k).wait_send())
        each(1, peers, lambda k: wspread(k, me).wait_send())
    for store in stores:
        store.wait()


def per_device(features, weight, tiles, tile_rows, tile_sources, send_blocks, cotangent):
    domains = lax.axis_size("dom")
    members = lax.axis_size("blk")
    peers = domains * members
    count, size = tiles.shape[2], tiles.shape[-1]
    own = features.shape[0] // size
    width, hidden = weight.shape
    nodes = own * size
    sum_here = width % (8 * peers) == 0
    scale = 1.0 / math.sqrt(nodes * peers)
    piece = width // peers if sum_here else 8
    pieces = peers - 1 if sum_here else 1
    halos = max(domains - 1, 1)
    others = max(members - 1, 1)
    vmem = pltpu.VMEM
    smem = pl.BlockSpec(memory_space=pltpu.SMEM)
    anywhere = pl.BlockSpec(memory_space=pl.ANY)
    activations, feature_grad, weight_grad = pl.pallas_call(
        functools.partial(kernel, domains, members, sum_here, scale),
        out_shape=(
            jax.ShapeDtypeStruct((nodes, hidden), BF16),
            jax.ShapeDtypeStruct((own, size, width), BF16),
            jax.ShapeDtypeStruct((width, hidden), F32),
        ),
        in_specs=[smem] * 3 + [anywhere] * 4,
        out_specs=(anywhere,) * 3,
        scratch_shapes=[
            vmem((own, size, width), BF16),
            vmem((width, hidden), BF16),
            vmem((count, size, size), BF16),
            vmem((count, size, size), BF16),
            vmem((nodes, hidden), BF16),
            vmem((own + domains, size, width), BF16),
            vmem((halos, size, width), BF16),
            vmem((count + 1, size, width), F32),
            pltpu.SMEM((max(own * members, own + domains),), jnp.int32),
            vmem((others, own, size, width), BF16),
            vmem((others, own, size, width), BF16),
            vmem((nodes, hidden), BF16),
            vmem((own * members, size, width), BF16),
            vmem((halos, size, width), BF16),
            vmem((halos, size, width), BF16),
            vmem((own, size, width), F32),
            vmem((width, hidden), F32),
            vmem((pieces, piece, hidden), F32),
            vmem((width, hidden), F32),
            DMA((8,)),
            DMA((halos,)), DMA((halos,)),
            DMA((others,)), DMA((others,)),
            DMA((others,)), DMA((others,)),
            DMA((halos,)), DMA((halos,)),
            DMA((pieces,)), DMA((pieces,)),
            DMA((pieces,)), DMA((pieces,)),
        ],
        compiler_params=pltpu.CompilerParams(
            collective_id=0, has_side_effects=True, vmem_limit_bytes=40 * 1024 * 1024),
    )(tile_rows, tile_sources, send_blocks, features.reshape(own, size, width), weight, tiles, cotangent)
    if not sum_here:
        weight_grad = lax.psum(weight_grad, ("dom", "blk"))
    return activations, feature_grad.reshape(nodes, width), weight_grad


def solution(mesh):
    return jax.shard_map(
        per_device,
        mesh=mesh,
        in_specs=(
            P(("groups", "dom", "blk"), None),
            P(),
            P(("groups", "dom"), "blk", None, None, None),
            P(("groups", "dom"), "blk", None),
            P(("groups", "dom"), "blk", None),
            P(("groups", "dom"), "blk", None),
            P(("groups", "dom", "blk"), None),
        ),
        out_specs=(
            P(("groups", "dom", "blk"), None),
            P(("groups", "dom", "blk"), None),
            P("groups", None),
        ),
        check_vma=False,
    )
```

```python
import functools
import math

import jax
import jax.numpy as jnp
from jax import lax
from jax.experimental import pallas as pl
from jax.experimental.pallas import tpu as pltpu
from jax.sharding import PartitionSpec as P

MESH = pl.DeviceIdType.MESH
BF16 = jnp.bfloat16
F32 = jnp.float32
DMA = pltpu.SemaphoreType.DMA


def each(low, high, step):
    if high - low <= 16:
        for i in range(low, high):
            step(i)
    else:
        lax.fori_loop(low, high, lambda i, c: (step(i), c)[1], 0)


def chain(keys, key_count, none):
    before = []
    for t, key in enumerate(keys):
        found = none
        for u in range(t):
            found = jnp.where(keys[u] == key, u, found)
        before.append(found)
    last = []
    for r in range(key_count):
        found = none
        for t, key in enumerate(keys):
            found = jnp.where(key == r, t, found)
        last.append(found)
    return before, last


def kernel(
    domains, members, sum_here, scale,
    rows_ref, sources_ref, chosen_ref, feat_hbm, weight_hbm, tiles_hbm, cot_hbm,
    act_hbm, fgrad_hbm, wgrad_hbm,
    feat, weight, tiles, tiles_t, cot, slots, outgoing, acc, last_ref, pair_out, pair_in, rs_out, rs_in,
    act, dom_h, ret_out, ret_in, fgrad, wown, wsend, wrecv, wzone, wzrecv, wgrad,
    local_sem, halo_send, halo_recv, pair_send, pair_recv, rs_send, rs_recv, ag_send, ag_recv,
    fw_send, fw_recv, ret_send, ret_recv, wb_send, wb_recv, wd_send, wd_recv,
    gb_send, gb_recv,
):
    own, size, width = feat.shape
    count = tiles.shape[0]
    d = lax.axis_index("dom")
    b = lax.axis_index("blk")
    pairs = members // 2
    chunks = rs_send.shape[1]
    span = own // chunks
    pair, side = lax.div(b, 2), lax.rem(b, 2)
    partner = b + 1 - 2 * side

    def dom_at(k):
        return lax.rem(d + k, domains)

    def blk_at(k):
        return lax.rem(b + k, members)

    def member(k, which):
        return 2 * lax.rem(pair + k, pairs) + which

    loads = [
        pltpu.make_async_copy(feat_hbm, feat, local_sem.at[0]),
        pltpu.make_async_copy(feat_hbm, slots.at[pl.ds(0, own)], local_sem.at[1]),
        pltpu.make_async_copy(tiles_hbm.at[0, 0], tiles, local_sem.at[2]),
        pltpu.make_async_copy(weight_hbm, weight, local_sem.at[3]),
        pltpu.make_async_copy(cot_hbm, cot, local_sem.at[4]),
    ]
    for load in loads:
        load.start()

    barrier = pltpu.get_barrier_semaphore()
    each(1, domains, lambda k: pl.semaphore_signal(
        barrier, inc=1, device_id={"dom": dom_at(k)}, device_id_type=MESH))
    each(1, members, lambda k: pl.semaphore_signal(
        barrier, inc=1, device_id={"blk": blk_at(k)}, device_id_type=MESH))

    loads[0].wait()

    def pick(k):
        outgoing[k - 1] = feat[jnp.minimum(chosen_ref[0, 0, dom_at(k)], own - 1)]

    each(1, domains, pick)
    pl.semaphore_wait(barrier, domains + members - 2)

    def halo(k):
        return pltpu.make_async_remote_copy(
            outgoing.at[k - 1], slots.at[own + d], halo_send.at[k - 1], halo_recv.at[k - 1],
            device_id={"dom": dom_at(k)}, device_id_type=MESH)

    def halo_in(k):
        return pltpu.make_async_remote_copy(
            outgoing.at[k - 1], slots.at[own + dom_at(domains - k)], halo_send.at[k - 1],
            halo_recv.at[k - 1], device_id={"dom": dom_at(k)}, device_id_type=MESH)

    each(1, domains, lambda k: halo(k).start())

    rows = [rows_ref[0, 0, t] for t in range(count)]
    sources = [sources_ref[0, 0, t] for t in range(count)]
    before, last = chain(rows, own * members, count)
    for r, value in enumerate(last):
        last_ref[r] = value
    acc[count] = jnp.zeros((size, width), F32)
    slots[own + d] = jnp.zeros((size, width), BF16)
    for load in loads[1:]:
        load.wait()
    each(1, domains, lambda k: halo_in(k).wait_recv())

    for t in range(count):
        product = jnp.dot(tiles[t], slots[sources[t]], preferred_element_type=F32)
        acc[t] = product + acc[before[t]]

    def remote(src, dst, send, recv, blk):
        return pltpu.make_async_remote_copy(
            src, dst, send, recv, device_id={"blk": blk}, device_id_type=MESH)

    def to_partner(k, c):
        part = pl.ds(c * span, span)
        return remote(pair_out.at[k, part], pair_in.at[k, part], pair_send.at[k, c],
                      pair_recv.at[k, c], partner)

    def across(k, c):
        part = pl.ds(c * span, span)
        return remote(rs_out.at[k - 1, part], rs_in.at[k - 1, part], rs_send.at[k - 1, c],
                      rs_recv.at[k - 1, c], member(k, side))

    order = [(k, c) for k in [*range(1, pairs), 0] for c in range(chunks)]
    for k, c in order:
        for s in range(c * span, (c + 1) * span):
            pair_out[k, s] = acc[last_ref[member(k, 1 - side) * own + s]].astype(BF16)
        to_partner(k, c).start()
    for k, c in order:
        if k:
            to_partner(k, c).wait_recv()
            for s in range(c * span, (c + 1) * span):
                rs_out[k - 1, s] = (
                    acc[last_ref[member(k, side) * own + s]] + pair_in[k, s].astype(F32)
                ).astype(BF16)
            across(k, c).start()

    before, last = chain(sources, own + domains, count)
    for t in range(count):
        tiles_t[t] = tiles[t].T

    def own_part(c):
        return dom_h.at[pl.ds(b * own + c * span, span)]

    def over(k, c):
        return remote(own_part(c), own_part(c), ag_send.at[k - 1, c], ag_recv.at[k - 1, c],
                      member(k, side))

    def held(k, c, which):
        return dom_h.at[pl.ds(member(pairs - k, which) * own + c * span, span)]

    def over_in(k, c):
        return remote(own_part(c), held(k, c, side), ag_send.at[k - 1, c], ag_recv.at[k - 1, c],
                      member(k, side))

    def forward(k, c):
        return remote(held(k, c, side), held(k, c, side), fw_send.at[k, c], fw_recv.at[k, c],
                      partner)

    def forward_in(k, c):
        return remote(held(k, c, side), held(k, c, 1 - side), fw_send.at[k, c], fw_recv.at[k, c],
                      partner)

    wpart = jnp.zeros(wown.shape, F32)
    later = []
    for c in range(chunks):
        to_partner(0, c).wait_recv()
        total = jnp.concatenate(
            [acc[last_ref[b * own + s]] + pair_in[0, s].astype(F32)
             for s in range(c * span, (c + 1) * span)], axis=0)
        for k in range(1, pairs):
            across(k, c).wait_recv()
            total += rs_in[k - 1, pl.ds(c * span, span)].reshape(span * size, width).astype(F32)
        gathered = total.astype(BF16)
        z = jnp.dot(gathered, weight[...], preferred_element_type=F32)
        sig = jax.nn.sigmoid(z)
        nodes = pl.ds(c * span * size, span * size)
        grad = (cot[nodes, :].astype(F32) * sig * (1.0 + z * (1.0 - sig))).astype(BF16)
        h = lax.dot_general(
            grad, weight[...], (((1,), (1,)), ((), ())), preferred_element_type=F32).astype(BF16)
        dom_h[pl.ds(b * own + c * span, span)] = h.reshape(span, size, width)
        for k in range(1, pairs):
            over(k, c).start()
        forward(0, c).start()
        act[nodes, :] = (z * sig).astype(BF16)
        later.append((gathered, grad))
    stores = [pltpu.make_async_copy(act, act_hbm, local_sem.at[5])]
    stores[0].start()
    for gathered, grad in later:
        wpart += lax.dot_general(
            gathered, grad, (((0,), (0,)), ((), ())), preferred_element_type=F32)
    wown[...] = wpart
    band = width // members
    mine = pl.ds(pl.multiple_of(b * band, 8), band)

    def wblk(m):
        rows_at = pl.ds(pl.multiple_of(blk_at(m) * band, 16), band)
        return remote(wsend.at[rows_at], wrecv.at[m - 1], wb_send.at[m - 1], wb_recv.at[m - 1],
                      blk_at(m))

    def wdom(k):
        return pltpu.make_async_remote_copy(
            wzone, wzrecv.at[k - 1], wd_send.at[k - 1], wd_recv.at[k - 1],
            device_id={"dom": dom_at(k)}, device_id_type=MESH)

    def gblk(m, who):
        at = pl.ds(pl.multiple_of(who * band, 8), band)
        return remote(wgrad.at[at], wgrad.at[at], gb_send.at[m - 1], gb_recv.at[m - 1], blk_at(m))

    if sum_here:
        wsend[...] = wpart.astype(BF16)
        for m in range(1, members):
            wblk(m).start()
    else:
        wgrad[...] = wpart * scale

    for c in range(chunks):
        for k in range(1, pairs):
            over_in(k, c).wait_recv()
            forward(k, c).start()
    for c in range(chunks):
        for k in range(pairs):
            forward_in(k, c).wait_recv()
    for t in range(count):
        product = jnp.dot(tiles_t[t], dom_h[rows[t]], preferred_element_type=F32)
        acc[t] = product + acc[before[t]]
    for s, value in enumerate(last):
        last_ref[s] = value

    if sum_here:
        summed = wown[mine, :]
        for m in range(1, members):
            wblk(m).wait_recv()
            summed += wrecv[m - 1].astype(F32)
        wzone[...] = summed.astype(BF16)
        each(1, domains, lambda k: wdom(k).start())

    def give_back(k):
        return pltpu.make_async_remote_copy(
            ret_out.at[k - 1], ret_in.at[k - 1], ret_send.at[k - 1], ret_recv.at[k - 1],
            device_id={"dom": dom_at(k)}, device_id_type=MESH)

    def give(k):
        ret_out[k - 1] = acc[last_ref[own + dom_at(k)]].astype(BF16)
        give_back(k).start()

    each(1, domains, give)

    if sum_here:
        summed = wzone[...].astype(F32)
        for k in range(1, domains):
            wdom(k).wait_recv()
            summed += wzrecv[k - 1].astype(F32)
        wgrad[mine, :] = summed * scale
        for m in range(1, members):
            gblk(m, b).start()

    for s in range(own):
        fgrad[s] = acc[last_ref[s]]

    def land(k):
        give_back(k).wait_recv()
        block = chosen_ref[0, 0, dom_at(domains - k)]
        value = ret_in[k - 1].astype(F32)
        for s in range(own):
            fgrad[s] += jnp.where(block == s, value, 0.0)

    each(1, domains, land)
    feat[...] = fgrad[...].astype(BF16)
    stores.append(pltpu.make_async_copy(feat, fgrad_hbm, local_sem.at[6]))
    stores[1].start()

    if sum_here:
        for m in range(1, members):
            gblk(m, blk_at(members - m)).wait_recv()
    stores.append(pltpu.make_async_copy(wgrad, wgrad_hbm, local_sem.at[7]))
    stores[2].start()

    each(1, domains, lambda k: halo(k).wait_send())
    each(1, domains, lambda k: give_back(k).wait_send())
    for c in range(chunks):
        for k in range(pairs):
            to_partner(k, c).wait_send()
            forward(k, c).wait_send()
            if k:
                across(k, c).wait_send()
                over(k, c).wait_send()
    if sum_here:
        each(1, domains, lambda k: wdom(k).wait_send())
        for m in range(1, members):
            wblk(m).wait_send()
            gblk(m, b).wait_send()
    for store in stores:
        store.wait()


def per_device(features, weight, tiles, tile_rows, tile_sources, send_blocks, cotangent):
    domains = lax.axis_size("dom")
    members = lax.axis_size("blk")
    peers = domains * members
    count, size = tiles.shape[2], tiles.shape[-1]
    own = features.shape[0] // size
    width, hidden = weight.shape
    nodes = own * size
    sum_here = width % (8 * peers) == 0
    scale = 1.0 / math.sqrt(nodes * peers)
    band = width // members
    zones = domains - 1 if sum_here and domains > 1 else 1
    halos = max(domains - 1, 1)
    others = max(members - 1, 1)
    pairs = members // 2
    far = max(pairs - 1, 1)
    chunks = 2 if own % 2 == 0 else 1
    vmem = pltpu.VMEM
    smem = pl.BlockSpec(memory_space=pltpu.SMEM)
    anywhere = pl.BlockSpec(memory_space=pl.ANY)
    activations, feature_grad, weight_grad = pl.pallas_call(
        functools.partial(kernel, domains, members, sum_here, scale),
        out_shape=(
            jax.ShapeDtypeStruct((nodes, hidden), BF16),
            jax.ShapeDtypeStruct((own, size, width), BF16),
            jax.ShapeDtypeStruct((width, hidden), F32),
        ),
        in_specs=[smem] * 3 + [anywhere] * 4,
        out_specs=(anywhere,) * 3,
        scratch_shapes=[
            vmem((own, size, width), BF16),
            vmem((width, hidden), BF16),
            vmem((count, size, size), BF16),
            vmem((count, size, size), BF16),
            vmem((nodes, hidden), BF16),
            vmem((own + domains, size, width), BF16),
            vmem((halos, size, width), BF16),
            vmem((count + 1, size, width), F32),
            pltpu.SMEM((max(own * members, own + domains),), jnp.int32),
            vmem((pairs, own, size, width), BF16),
            vmem((pairs, own, size, width), BF16),
            vmem((far, own, size, width), BF16),
            vmem((far, own, size, width), BF16),
            vmem((nodes, hidden), BF16),
            vmem((own * members, size, width), BF16),
            vmem((halos, size, width), BF16),
            vmem((halos, size, width), BF16),
            vmem((own, size, width), F32),
            vmem((width, hidden), F32),
            vmem((width, hidden), BF16),
            vmem((others, band, hidden), BF16),
            vmem((band, hidden), BF16),
            vmem((zones, band, hidden), BF16),
            vmem((width, hidden), F32),
            DMA((8,)),
            DMA((halos,)), DMA((halos,)),
            DMA((pairs, chunks)), DMA((pairs, chunks)),
            DMA((far, chunks)), DMA((far, chunks)),
            DMA((far, chunks)), DMA((far, chunks)),
            DMA((pairs, chunks)), DMA((pairs, chunks)),
            DMA((halos,)), DMA((halos,)),
            DMA((others,)), DMA((others,)),
            DMA((zones,)), DMA((zones,)),
            DMA((others,)), DMA((others,)),
        ],
        compiler_params=pltpu.CompilerParams(
            collective_id=0, has_side_effects=True, vmem_limit_bytes=55 * 1024 * 1024),
    )(tile_rows, tile_sources, send_blocks, features.reshape(own, size, width), weight, tiles, cotangent)
    if not sum_here:
        weight_grad = lax.psum(weight_grad, ("dom", "blk"))
    return activations, feature_grad.reshape(nodes, width), weight_grad


def solution(mesh):
    return jax.shard_map(
        per_device,
        mesh=mesh,
        in_specs=(
            P(("groups", "dom", "blk"), None),
            P(),
            P(("groups", "dom"), "blk", None, None, None),
            P(("groups", "dom"), "blk", None),
            P(("groups", "dom"), "blk", None),
            P(("groups", "dom"), "blk", None),
            P(("groups", "dom", "blk"), None),
        ),
        out_specs=(
            P(("groups", "dom", "blk"), None),
            P(("groups", "dom", "blk"), None),
            P("groups", None),
        ),
        check_vma=False,
    )
```

```python
import functools
import math

import jax
import jax.numpy as jnp
from jax import lax
from jax.experimental import pallas as pl
from jax.experimental.pallas import tpu as pltpu
from jax.sharding import PartitionSpec as P

MESH = pl.DeviceIdType.MESH
BF16 = jnp.bfloat16
F32 = jnp.float32
DMA = pltpu.SemaphoreType.DMA


def each(low, high, step):
    if high - low <= 16:
        for i in range(low, high):
            step(i)
    else:
        lax.fori_loop(low, high, lambda i, c: (step(i), c)[1], 0)


def chain(keys, key_count, none):
    before = []
    for t, key in enumerate(keys):
        found = none
        for u in range(t):
            found = jnp.where(keys[u] == key, u, found)
        before.append(found)
    last = []
    for r in range(key_count):
        found = none
        for t, key in enumerate(keys):
            found = jnp.where(key == r, t, found)
        last.append(found)
    return before, last


def kernel(
    domains, members, sum_here, scale,
    rows_ref, sources_ref, chosen_ref, feat_hbm, weight_hbm, tiles_hbm, cot_hbm,
    act, fgrad_out, wgrad_out,
    feat, weight, tiles, tiles_t, cot, slots, outgoing, acc, last_ref, pair_out, pair_in, rs_out, rs_in,
    dom_h, ret_out, ret_in, fgrad, wown, wsend, wrecv, wzone, wzrecv, wgrad,
    local_sem, halo_send, halo_recv, pair_send, pair_recv, rs_send, rs_recv, ag_send, ag_recv,
    fw_send, fw_recv, ret_send, ret_recv, wb_send, wb_recv, wd_send, wd_recv,
    gb_send, gb_recv,
):
    own, size, width = feat.shape
    count = tiles.shape[0]
    d = lax.axis_index("dom")
    b = lax.axis_index("blk")
    pairs = members // 2
    chunks = rs_send.shape[1]
    span = own // chunks
    pair, side = lax.div(b, 2), lax.rem(b, 2)
    partner = b + 1 - 2 * side

    def dom_at(k):
        return lax.rem(d + k, domains)

    def blk_at(k):
        return lax.rem(b + k, members)

    def member(k, which):
        return 2 * lax.rem(pair + k, pairs) + which

    loads = [
        pltpu.make_async_copy(feat_hbm, feat, local_sem.at[0]),
        pltpu.make_async_copy(feat_hbm, slots.at[pl.ds(0, own)], local_sem.at[1]),
        pltpu.make_async_copy(tiles_hbm.at[0, 0], tiles, local_sem.at[2]),
        pltpu.make_async_copy(weight_hbm, weight, local_sem.at[3]),
        pltpu.make_async_copy(cot_hbm, cot, local_sem.at[4]),
    ]
    for load in loads:
        load.start()

    barrier = pltpu.get_barrier_semaphore()
    each(1, domains, lambda k: pl.semaphore_signal(
        barrier, inc=1, device_id={"dom": dom_at(k)}, device_id_type=MESH))
    each(1, members, lambda k: pl.semaphore_signal(
        barrier, inc=1, device_id={"blk": blk_at(k)}, device_id_type=MESH))

    loads[0].wait()

    def pick(k):
        outgoing[k - 1] = feat[jnp.minimum(chosen_ref[0, 0, dom_at(k)], own - 1)]

    each(1, domains, pick)
    pl.semaphore_wait(barrier, domains + members - 2)

    def halo(k):
        return pltpu.make_async_remote_copy(
            outgoing.at[k - 1], slots.at[own + d], halo_send.at[k - 1], halo_recv.at[k - 1],
            device_id={"dom": dom_at(k)}, device_id_type=MESH)

    def halo_in(k):
        return pltpu.make_async_remote_copy(
            outgoing.at[k - 1], slots.at[own + dom_at(domains - k)], halo_send.at[k - 1],
            halo_recv.at[k - 1], device_id={"dom": dom_at(k)}, device_id_type=MESH)

    each(1, domains, lambda k: halo(k).start())

    rows = [rows_ref[0, 0, t] for t in range(count)]
    sources = [sources_ref[0, 0, t] for t in range(count)]
    before, last = chain(rows, own * members, count)
    for r, value in enumerate(last):
        last_ref[r] = value
    acc[count] = jnp.zeros((size, width), F32)
    slots[own + d] = jnp.zeros((size, width), BF16)
    for load in loads[1:]:
        load.wait()
    each(1, domains, lambda k: halo_in(k).wait_recv())

    for t in range(count):
        product = jnp.dot(tiles[t], slots[sources[t]], preferred_element_type=F32)
        acc[t] = product + acc[before[t]]

    def remote(src, dst, send, recv, blk):
        return pltpu.make_async_remote_copy(
            src, dst, send, recv, device_id={"blk": blk}, device_id_type=MESH)

    def to_partner(k, c):
        part = pl.ds(c * span, span)
        return remote(pair_out.at[k, part], pair_in.at[k, part], pair_send.at[k, c],
                      pair_recv.at[k, c], partner)

    def across(k, c):
        part = pl.ds(c * span, span)
        return remote(rs_out.at[k - 1, part], rs_in.at[k - 1, part], rs_send.at[k - 1, c],
                      rs_recv.at[k - 1, c], member(k, side))

    order = [(k, c) for k in [*range(1, pairs), 0] for c in range(chunks)]
    for k, c in order:
        for s in range(c * span, (c + 1) * span):
            pair_out[k, s] = acc[last_ref[member(k, 1 - side) * own + s]].astype(BF16)
        to_partner(k, c).start()
    for k, c in order:
        if k:
            to_partner(k, c).wait_recv()
            for s in range(c * span, (c + 1) * span):
                rs_out[k - 1, s] = (
                    acc[last_ref[member(k, side) * own + s]] + pair_in[k, s].astype(F32)
                ).astype(BF16)
            across(k, c).start()

    before, last = chain(sources, own + domains, count)
    for t in range(count):
        tiles_t[t] = tiles[t].T

    def own_part(c):
        return dom_h.at[pl.ds(b * own + c * span, span)]

    def over(k, c):
        return remote(own_part(c), own_part(c), ag_send.at[k - 1, c], ag_recv.at[k - 1, c],
                      member(k, side))

    def held(k, c, which):
        return dom_h.at[pl.ds(member(pairs - k, which) * own + c * span, span)]

    def over_in(k, c):
        return remote(own_part(c), held(k, c, side), ag_send.at[k - 1, c], ag_recv.at[k - 1, c],
                      member(k, side))

    def forward(k, c):
        return remote(held(k, c, side), held(k, c, side), fw_send.at[k, c], fw_recv.at[k, c],
                      partner)

    def forward_in(k, c):
        return remote(held(k, c, side), held(k, c, 1 - side), fw_send.at[k, c], fw_recv.at[k, c],
                      partner)

    wpart = jnp.zeros(wown.shape, F32)
    later = []
    for c in range(chunks):
        to_partner(0, c).wait_recv()
        total = jnp.concatenate(
            [acc[last_ref[b * own + s]] + pair_in[0, s].astype(F32)
             for s in range(c * span, (c + 1) * span)], axis=0)
        for k in range(1, pairs):
            across(k, c).wait_recv()
            total += rs_in[k - 1, pl.ds(c * span, span)].reshape(span * size, width).astype(F32)
        gathered = total.astype(BF16)
        z = jnp.dot(gathered, weight[...], preferred_element_type=F32)
        sig = jax.nn.sigmoid(z)
        nodes = pl.ds(c * span * size, span * size)
        grad = (cot[nodes, :].astype(F32) * sig * (1.0 + z * (1.0 - sig))).astype(BF16)
        h = lax.dot_general(
            grad, weight[...], (((1,), (1,)), ((), ())), preferred_element_type=F32).astype(BF16)
        dom_h[pl.ds(b * own + c * span, span)] = h.reshape(span, size, width)
        for k in range(1, pairs):
            over(k, c).start()
        forward(0, c).start()
        act[nodes, :] = (z * sig).astype(BF16)
        later.append((gathered, grad))
    for gathered, grad in later:
        wpart += lax.dot_general(
            gathered, grad, (((0,), (0,)), ((), ())), preferred_element_type=F32)
    wown[...] = wpart
    band = width // members
    mine = pl.ds(pl.multiple_of(b * band, 8), band)

    def wblk(m):
        rows_at = pl.ds(pl.multiple_of(blk_at(m) * band, 16), band)
        return remote(wsend.at[rows_at], wrecv.at[m - 1], wb_send.at[m - 1], wb_recv.at[m - 1],
                      blk_at(m))

    def wdom(k):
        return pltpu.make_async_remote_copy(
            wzone, wzrecv.at[k - 1], wd_send.at[k - 1], wd_recv.at[k - 1],
            device_id={"dom": dom_at(k)}, device_id_type=MESH)

    def gblk(m, who):
        at = pl.ds(pl.multiple_of(who * band, 8), band)
        return remote(wgrad.at[at], wgrad.at[at], gb_send.at[m - 1], gb_recv.at[m - 1], blk_at(m))

    if sum_here:
        wsend[...] = wpart.astype(BF16)
        for m in range(1, members):
            wblk(m).start()
    else:
        wgrad[...] = wpart * scale

    for c in range(chunks):
        for k in range(1, pairs):
            over_in(k, c).wait_recv()
            forward(k, c).start()
    if sum_here:
        summed = wown[mine, :]
        for m in range(1, members):
            wblk(m).wait_recv()
            summed += wrecv[m - 1].astype(F32)
        wzone[...] = summed.astype(BF16)
        each(1, domains, lambda k: wdom(k).start())

    for c in range(chunks):
        for k in range(pairs):
            forward_in(k, c).wait_recv()
    for t in range(count):
        product = jnp.dot(tiles_t[t], dom_h[rows[t]], preferred_element_type=F32)
        acc[t] = product + acc[before[t]]
    for s, value in enumerate(last):
        last_ref[s] = value

    def give_back(k):
        return pltpu.make_async_remote_copy(
            ret_out.at[k - 1], ret_in.at[k - 1], ret_send.at[k - 1], ret_recv.at[k - 1],
            device_id={"dom": dom_at(k)}, device_id_type=MESH)

    def give(k):
        ret_out[k - 1] = acc[last_ref[own + dom_at(k)]].astype(BF16)
        give_back(k).start()

    each(1, domains, give)

    if sum_here:
        summed = wzone[...].astype(F32)
        for k in range(1, domains):
            wdom(k).wait_recv()
            summed += wzrecv[k - 1].astype(F32)
        wgrad[mine, :] = summed * scale
        for m in range(1, members):
            gblk(m, b).start()

    for s in range(own):
        fgrad[s] = acc[last_ref[s]]

    def land(k):
        give_back(k).wait_recv()
        block = chosen_ref[0, 0, dom_at(domains - k)]
        value = ret_in[k - 1].astype(F32)
        for s in range(own):
            fgrad[s] += jnp.where(block == s, value, 0.0)

    each(1, domains, land)
    fgrad_out[...] = fgrad[...].astype(BF16)

    if sum_here:
        for m in range(1, members):
            gblk(m, blk_at(members - m)).wait_recv()
    wgrad_out[...] = wgrad[...]

    each(1, domains, lambda k: halo(k).wait_send())
    each(1, domains, lambda k: give_back(k).wait_send())
    for c in range(chunks):
        for k in range(pairs):
            to_partner(k, c).wait_send()
            forward(k, c).wait_send()
            if k:
                across(k, c).wait_send()
                over(k, c).wait_send()
    if sum_here:
        each(1, domains, lambda k: wdom(k).wait_send())
        for m in range(1, members):
            wblk(m).wait_send()
            gblk(m, b).wait_send()


def per_device(features, weight, tiles, tile_rows, tile_sources, send_blocks, cotangent):
    domains = lax.axis_size("dom")
    members = lax.axis_size("blk")
    peers = domains * members
    count, size = tiles.shape[2], tiles.shape[-1]
    own = features.shape[0] // size
    width, hidden = weight.shape
    nodes = own * size
    sum_here = width % (8 * peers) == 0
    scale = 1.0 / math.sqrt(nodes * peers)
    band = width // members
    zones = domains - 1 if sum_here and domains > 1 else 1
    halos = max(domains - 1, 1)
    others = max(members - 1, 1)
    pairs = members // 2
    far = max(pairs - 1, 1)
    chunks = own
    vmem = pltpu.VMEM
    smem = pl.BlockSpec(memory_space=pltpu.SMEM)
    anywhere = pl.BlockSpec(memory_space=pl.ANY)
    activations, feature_grad, weight_grad = pl.pallas_call(
        functools.partial(kernel, domains, members, sum_here, scale),
        out_shape=(
            vmem((nodes, hidden), BF16),
            vmem((own, size, width), BF16),
            vmem((width, hidden), F32),
        ),
        in_specs=[smem] * 3 + [anywhere] * 4,
        out_specs=(pl.BlockSpec(memory_space=pltpu.VMEM),) * 3,
        scratch_shapes=[
            vmem((own, size, width), BF16),
            vmem((width, hidden), BF16),
            vmem((count, size, size), BF16),
            vmem((count, size, size), BF16),
            vmem((nodes, hidden), BF16),
            vmem((own + domains, size, width), BF16),
            vmem((halos, size, width), BF16),
            vmem((count + 1, size, width), F32),
            pltpu.SMEM((max(own * members, own + domains),), jnp.int32),
            vmem((pairs, own, size, width), BF16),
            vmem((pairs, own, size, width), BF16),
            vmem((far, own, size, width), BF16),
            vmem((far, own, size, width), BF16),
            vmem((own * members, size, width), BF16),
            vmem((halos, size, width), BF16),
            vmem((halos, size, width), BF16),
            vmem((own, size, width), F32),
            vmem((width, hidden), F32),
            vmem((width, hidden), BF16),
            vmem((others, band, hidden), BF16),
            vmem((band, hidden), BF16),
            vmem((zones, band, hidden), BF16),
            vmem((width, hidden), F32),
            DMA((5,)),
            DMA((halos,)), DMA((halos,)),
            DMA((pairs, chunks)), DMA((pairs, chunks)),
            DMA((far, chunks)), DMA((far, chunks)),
            DMA((far, chunks)), DMA((far, chunks)),
            DMA((pairs, chunks)), DMA((pairs, chunks)),
            DMA((halos,)), DMA((halos,)),
            DMA((others,)), DMA((others,)),
            DMA((zones,)), DMA((zones,)),
            DMA((others,)), DMA((others,)),
        ],
        compiler_params=pltpu.CompilerParams(
            collective_id=0, has_side_effects=True, vmem_limit_bytes=58 * 1024 * 1024),
    )(tile_rows, tile_sources, send_blocks, features.reshape(own, size, width), weight, tiles, cotangent)
    if not sum_here:
        weight_grad = lax.psum(weight_grad, ("dom", "blk"))
    return activations, feature_grad.reshape(nodes, width), weight_grad


def solution(mesh):
    return jax.shard_map(
        per_device,
        mesh=mesh,
        in_specs=(
            P(("groups", "dom", "blk"), None),
            P(),
            P(("groups", "dom"), "blk", None, None, None),
            P(("groups", "dom"), "blk", None),
            P(("groups", "dom"), "blk", None),
            P(("groups", "dom"), "blk", None),
            P(("groups", "dom", "blk"), None),
        ),
        out_specs=(
            P(("groups", "dom", "blk"), None),
            P(("groups", "dom", "blk"), None),
            P("groups", None),
        ),
        check_vma=False,
    )
```

```python
import functools
import math

import jax
import jax.numpy as jnp
from jax import lax
from jax.experimental import pallas as pl
from jax.experimental.pallas import tpu as pltpu
from jax.sharding import PartitionSpec as P

MESH = pl.DeviceIdType.MESH
BF16 = jnp.bfloat16
F32 = jnp.float32
DMA = pltpu.SemaphoreType.DMA


def each(low, high, step):
    if high - low <= 16:
        for i in range(low, high):
            step(i)
    else:
        lax.fori_loop(low, high, lambda i, c: (step(i), c)[1], 0)


def chain(keys, key_count, none):
    before = []
    for t, key in enumerate(keys):
        found = none
        for u in range(t):
            found = jnp.where(keys[u] == key, u, found)
        before.append(found)
    last = []
    for r in range(key_count):
        found = none
        for t, key in enumerate(keys):
            found = jnp.where(key == r, t, found)
        last.append(found)
    return before, last


def kernel(
    domains, members, sum_here, scale,
    rows_ref, sources_ref, chosen_ref, feat_hbm, weight_hbm, tiles_hbm, cot_hbm,
    act, fgrad_out, wgrad_out,
    feat, weight, tiles, tiles_t, cot, slots, outgoing, acc, last_ref, pair_out, pair_in, rs_out, rs_in,
    dom_h, ret_out, ret_in, fgrad, wown, wsend, wrecv, wzone, wzrecv, wgrad,
    local_sem, halo_send, halo_recv, pair_send, pair_recv, rs_send, rs_recv, ag_send, ag_recv,
    fw_send, fw_recv, ret_send, ret_recv, wb_send, wb_recv, wd_send, wd_recv,
    gb_send, gb_recv,
):
    own, size, width = feat.shape
    count = tiles.shape[0]
    d = lax.axis_index("dom")
    b = lax.axis_index("blk")
    pairs = members // 2
    chunks = rs_send.shape[1]
    span = own // chunks
    pair, side = lax.div(b, 2), lax.rem(b, 2)
    partner = b + 1 - 2 * side

    def dom_at(k):
        return lax.rem(d + k, domains)

    def blk_at(k):
        return lax.rem(b + k, members)

    def member(k, which):
        return 2 * lax.rem(pair + k, pairs) + which

    loads = [
        pltpu.make_async_copy(feat_hbm, feat, local_sem.at[0]),
        pltpu.make_async_copy(feat_hbm, slots.at[pl.ds(0, own)], local_sem.at[1]),
        pltpu.make_async_copy(tiles_hbm.at[0, 0], tiles, local_sem.at[2]),
        pltpu.make_async_copy(weight_hbm, weight, local_sem.at[3]),
        pltpu.make_async_copy(cot_hbm, cot, local_sem.at[4]),
    ]
    for load in loads:
        load.start()

    barrier = pltpu.get_barrier_semaphore()
    each(1, domains, lambda k: pl.semaphore_signal(
        barrier, inc=1, device_id={"dom": dom_at(k)}, device_id_type=MESH))
    each(1, members, lambda k: pl.semaphore_signal(
        barrier, inc=1, device_id={"blk": blk_at(k)}, device_id_type=MESH))

    loads[0].wait()

    def pick(k):
        outgoing[k - 1] = feat[jnp.minimum(chosen_ref[0, 0, dom_at(k)], own - 1)]

    each(1, domains, pick)
    pl.semaphore_wait(barrier, domains + members - 2)

    def halo(k):
        return pltpu.make_async_remote_copy(
            outgoing.at[k - 1], slots.at[own + d], halo_send.at[k - 1], halo_recv.at[k - 1],
            device_id={"dom": dom_at(k)}, device_id_type=MESH)

    def halo_in(k):
        return pltpu.make_async_remote_copy(
            outgoing.at[k - 1], slots.at[own + dom_at(domains - k)], halo_send.at[k - 1],
            halo_recv.at[k - 1], device_id={"dom": dom_at(k)}, device_id_type=MESH)

    each(1, domains, lambda k: halo(domains - k).start())

    rows = [rows_ref[0, 0, t] for t in range(count)]
    sources = [sources_ref[0, 0, t] for t in range(count)]
    before, last = chain(rows, own * members, count)
    for r, value in enumerate(last):
        last_ref[r] = value
    acc[count] = jnp.zeros((size, width), F32)
    slots[own + d] = jnp.zeros((size, width), BF16)
    for load in loads[1:]:
        load.wait()
    each(1, domains, lambda k: halo_in(k).wait_recv())

    for t in range(count):
        product = jnp.dot(tiles[t], slots[sources[t]], preferred_element_type=F32)
        acc[t] = product + acc[before[t]]

    def remote(src, dst, send, recv, blk):
        return pltpu.make_async_remote_copy(
            src, dst, send, recv, device_id={"blk": blk}, device_id_type=MESH)

    def to_partner(k, c):
        part = pl.ds(c * span, span)
        return remote(pair_out.at[k, part], pair_in.at[k, part], pair_send.at[k, c],
                      pair_recv.at[k, c], partner)

    def across(k, c):
        part = pl.ds(c * span, span)
        return remote(rs_out.at[k - 1, part], rs_in.at[k - 1, part], rs_send.at[k - 1, c],
                      rs_recv.at[k - 1, c], member(k, side))

    order = [(k, c) for k in [*range(1, pairs), 0] for c in range(chunks)]
    for k, c in order:
        for s in range(c * span, (c + 1) * span):
            pair_out[k, s] = acc[last_ref[member(k, 1 - side) * own + s]].astype(BF16)
        to_partner(k, c).start()
    for k, c in order:
        if k:
            to_partner(k, c).wait_recv()
            for s in range(c * span, (c + 1) * span):
                rs_out[k - 1, s] = (
                    acc[last_ref[member(k, side) * own + s]] + pair_in[k, s].astype(F32)
                ).astype(BF16)
            across(k, c).start()

    before, last = chain(sources, own + domains, count)
    for t in range(count):
        tiles_t[t] = tiles[t].T

    def own_part(c):
        return dom_h.at[pl.ds(b * own + c * span, span)]

    def over(k, c):
        return remote(own_part(c), own_part(c), ag_send.at[k - 1, c], ag_recv.at[k - 1, c],
                      member(k, side))

    def held(k, c, which):
        return dom_h.at[pl.ds(member(pairs - k, which) * own + c * span, span)]

    def over_in(k, c):
        return remote(own_part(c), held(k, c, side), ag_send.at[k - 1, c], ag_recv.at[k - 1, c],
                      member(k, side))

    def forward(k, c):
        return remote(held(k, c, side), held(k, c, side), fw_send.at[k, c], fw_recv.at[k, c],
                      partner)

    def forward_in(k, c):
        return remote(held(k, c, side), held(k, c, 1 - side), fw_send.at[k, c], fw_recv.at[k, c],
                      partner)

    wpart = jnp.zeros(wown.shape, F32)
    later = []
    for c in range(chunks):
        to_partner(0, c).wait_recv()
        total = jnp.concatenate(
            [acc[last_ref[b * own + s]] + pair_in[0, s].astype(F32)
             for s in range(c * span, (c + 1) * span)], axis=0)
        for k in range(1, pairs):
            across(k, c).wait_recv()
            total += rs_in[k - 1, pl.ds(c * span, span)].reshape(span * size, width).astype(F32)
        gathered = total.astype(BF16)
        z = jnp.dot(gathered, weight[...], preferred_element_type=F32)
        sig = jax.nn.sigmoid(z)
        nodes = pl.ds(c * span * size, span * size)
        grad = (cot[nodes, :].astype(F32) * sig * (1.0 + z * (1.0 - sig))).astype(BF16)
        h = lax.dot_general(
            grad, weight[...], (((1,), (1,)), ((), ())), preferred_element_type=F32).astype(BF16)
        dom_h[pl.ds(b * own + c * span, span)] = h.reshape(span, size, width)
        for k in range(1, pairs):
            over(k, c).start()
        forward(0, c).start()
        act[nodes, :] = (z * sig).astype(BF16)
        later.append((gathered, grad))
    for gathered, grad in later:
        wpart += lax.dot_general(
            gathered, grad, (((0,), (0,)), ((), ())), preferred_element_type=F32)
    wown[...] = wpart
    band = width // members
    mine = pl.ds(pl.multiple_of(b * band, 8), band)

    def wblk(m):
        rows_at = pl.ds(pl.multiple_of(blk_at(m) * band, 16), band)
        return remote(wsend.at[rows_at], wrecv.at[m - 1], wb_send.at[m - 1], wb_recv.at[m - 1],
                      blk_at(m))

    def wdom(k):
        return pltpu.make_async_remote_copy(
            wzone, wzrecv.at[k - 1], wd_send.at[k - 1], wd_recv.at[k - 1],
            device_id={"dom": dom_at(k)}, device_id_type=MESH)

    def gblk(m, who):
        at = pl.ds(pl.multiple_of(who * band, 8), band)
        return remote(wgrad.at[at], wgrad.at[at], gb_send.at[m - 1], gb_recv.at[m - 1], blk_at(m))

    if sum_here:
        wsend[...] = wpart.astype(BF16)
        for m in range(1, members):
            wblk(m).start()
    else:
        wgrad[...] = wpart * scale

    for c in range(chunks):
        for k in range(1, pairs):
            over_in(k, c).wait_recv()
            forward(k, c).start()
    if sum_here:
        summed = wown[mine, :]
        for m in range(1, members):
            wblk(m).wait_recv()
            summed += wrecv[m - 1].astype(F32)
        wzone[...] = summed.astype(BF16)
        each(1, domains, lambda k: wdom(k).start())

    for c in range(chunks):
        for k in range(pairs):
            forward_in(k, c).wait_recv()
    for t in range(count):
        product = jnp.dot(tiles_t[t], dom_h[rows[t]], preferred_element_type=F32)
        acc[t] = product + acc[before[t]]
    for s, value in enumerate(last):
        last_ref[s] = value

    def give_back(k):
        return pltpu.make_async_remote_copy(
            ret_out.at[k - 1], ret_in.at[k - 1], ret_send.at[k - 1], ret_recv.at[k - 1],
            device_id={"dom": dom_at(k)}, device_id_type=MESH)

    def give(k):
        ret_out[k - 1] = acc[last_ref[own + dom_at(k)]].astype(BF16)
        give_back(k).start()

    each(1, domains, lambda k: give(domains - k))

    if sum_here:
        summed = wzone[...].astype(F32)
        for k in range(1, domains):
            wdom(k).wait_recv()
            summed += wzrecv[k - 1].astype(F32)
        wgrad[mine, :] = summed * scale
        for m in range(1, members):
            gblk(m, b).start()

    for s in range(own):
        fgrad[s] = acc[last_ref[s]]

    def land(k):
        give_back(k).wait_recv()
        block = chosen_ref[0, 0, dom_at(domains - k)]
        value = ret_in[k - 1].astype(F32)
        for s in range(own):
            fgrad[s] += jnp.where(block == s, value, 0.0)

    each(1, domains, land)
    fgrad_out[...] = fgrad[...].astype(BF16)

    if sum_here:
        for m in range(1, members):
            gblk(m, blk_at(members - m)).wait_recv()
    wgrad_out[...] = wgrad[...]

    each(1, domains, lambda k: halo(k).wait_send())
    each(1, domains, lambda k: give_back(k).wait_send())
    for c in range(chunks):
        for k in range(pairs):
            to_partner(k, c).wait_send()
            forward(k, c).wait_send()
            if k:
                across(k, c).wait_send()
                over(k, c).wait_send()
    if sum_here:
        each(1, domains, lambda k: wdom(k).wait_send())
        for m in range(1, members):
            wblk(m).wait_send()
            gblk(m, b).wait_send()


def per_device(features, weight, tiles, tile_rows, tile_sources, send_blocks, cotangent):
    domains = lax.axis_size("dom")
    members = lax.axis_size("blk")
    peers = domains * members
    count, size = tiles.shape[2], tiles.shape[-1]
    own = features.shape[0] // size
    width, hidden = weight.shape
    nodes = own * size
    sum_here = width % (8 * peers) == 0
    scale = 1.0 / math.sqrt(nodes * peers)
    band = width // members
    zones = domains - 1 if sum_here and domains > 1 else 1
    halos = max(domains - 1, 1)
    others = max(members - 1, 1)
    pairs = members // 2
    far = max(pairs - 1, 1)
    chunks = own
    vmem = pltpu.VMEM
    smem = pl.BlockSpec(memory_space=pltpu.SMEM)
    anywhere = pl.BlockSpec(memory_space=pl.ANY)
    activations, feature_grad, weight_grad = pl.pallas_call(
        functools.partial(kernel, domains, members, sum_here, scale),
        out_shape=(
            vmem((nodes, hidden), BF16),
            vmem((own, size, width), BF16),
            vmem((width, hidden), F32),
        ),
        in_specs=[smem] * 3 + [anywhere] * 4,
        out_specs=(pl.BlockSpec(memory_space=pltpu.VMEM),) * 3,
        scratch_shapes=[
            vmem((own, size, width), BF16),
            vmem((width, hidden), BF16),
            vmem((count, size, size), BF16),
            vmem((count, size, size), BF16),
            vmem((nodes, hidden), BF16),
            vmem((own + domains, size, width), BF16),
            vmem((halos, size, width), BF16),
            vmem((count + 1, size, width), F32),
            pltpu.SMEM((max(own * members, own + domains),), jnp.int32),
            vmem((pairs, own, size, width), BF16),
            vmem((pairs, own, size, width), BF16),
            vmem((far, own, size, width), BF16),
            vmem((far, own, size, width), BF16),
            vmem((own * members, size, width), BF16),
            vmem((halos, size, width), BF16),
            vmem((halos, size, width), BF16),
            vmem((own, size, width), F32),
            vmem((width, hidden), F32),
            vmem((width, hidden), BF16),
            vmem((others, band, hidden), BF16),
            vmem((band, hidden), BF16),
            vmem((zones, band, hidden), BF16),
            vmem((width, hidden), F32),
            DMA((5,)),
            DMA((halos,)), DMA((halos,)),
            DMA((pairs, chunks)), DMA((pairs, chunks)),
            DMA((far, chunks)), DMA((far, chunks)),
            DMA((far, chunks)), DMA((far, chunks)),
            DMA((pairs, chunks)), DMA((pairs, chunks)),
            DMA((halos,)), DMA((halos,)),
            DMA((others,)), DMA((others,)),
            DMA((zones,)), DMA((zones,)),
            DMA((others,)), DMA((others,)),
        ],
        compiler_params=pltpu.CompilerParams(
            collective_id=0, has_side_effects=True, vmem_limit_bytes=58 * 1024 * 1024),
    )(tile_rows, tile_sources, send_blocks, features.reshape(own, size, width), weight, tiles, cotangent)
    if not sum_here:
        weight_grad = lax.psum(weight_grad, ("dom", "blk"))
    return activations, feature_grad.reshape(nodes, width), weight_grad


def solution(mesh):
    return jax.shard_map(
        per_device,
        mesh=mesh,
        in_specs=(
            P(("groups", "dom", "blk"), None),
            P(),
            P(("groups", "dom"), "blk", None, None, None),
            P(("groups", "dom"), "blk", None),
            P(("groups", "dom"), "blk", None),
            P(("groups", "dom"), "blk", None),
            P(("groups", "dom", "blk"), None),
        ),
        out_specs=(
            P(("groups", "dom", "blk"), None),
            P(("groups", "dom", "blk"), None),
            P("groups", None),
        ),
        check_vma=False,
    )
```
